32 devices in a mesh: grp: 2 (over y), blk: 8 (over z, core), red: 2 (over x), sub: 1.
Axes of the slice: x: 2, y: 2, z: 4, core: 2. Of those that a mesh axis runs over, the one named last changes fastest.
Arguments:
- tokens: bfloat16 [256, 8192], P(('grp', 'blk'), ('red', 'sub')), parts along dimension 0, may hold values from -12 to 12
- input_gain: bfloat16 [8192], replicated, may hold values from 0.5 to 1.5
- in_weight: bfloat16 [2, 8192, 16384], P(None, None, ('blk', 'red', 'sub')), may hold values from -0.0625 to 0.0625
- conv_weight: bfloat16 [4, 16384], P(None, ('blk', 'red', 'sub')), may hold values from -2.5 to 2.5
- conv_bias: bfloat16 [16384], P(('blk', 'red', 'sub')), may hold values from -0.5 to 0.5
- param_weight: bfloat16 [16384, 544], P(('blk', 'red', 'sub')), may hold values from -0.046875 to 0.046875
- step_gain: bfloat16 [512], replicated, may hold values from 0.25 to 1.75
- entry_gain: bfloat16 [16], replicated, may hold values from 0.099609375 to 1.8984375
- readout_gain: bfloat16 [16], replicated, may hold values from 0.099609375 to 1.8984375
- step_weight: bfloat16 [512, 16384], P(None, ('blk', 'red', 'sub')), may hold values from -0.25 to 0.25
- step_bias: float32 [16384], P(('blk', 'red', 'sub')), may hold values from -2 to 0.5
- decay_log: float32 [16, 16384], P(None, ('blk', 'red', 'sub')), may hold values from 0 to 2.77
- skip_gain: float32 [16384], P(('blk', 'red', 'sub')), may hold values from 0.5 to 1.5
- out_weight: bfloat16 [16384, 8192], P('blk', ('red', 'sub')), may hold values from -0.046875 to 0.046875
- conv_state: bfloat16 [3, 16384, 256], P(None, ('blk', 'red', 'sub'), 'grp'), parts along dimension 2, may hold values from -5 to 5
- scan_state: bfloat16 [16384, 16, 256], P(('blk', 'red', 'sub'), None, 'grp'), parts along dimension 2, may hold values from -5 to 5
Outputs:
- mixed: bfloat16 [256, 8192], P(('grp', 'blk'), ('red', 'sub')), parts along dimension 0
- new_conv: bfloat16 [3, 16384, 256], P(None, ('blk', 'red', 'sub'), 'grp'), parts along dimension 2
- new_scan: bfloat16 [16384, 16, 256], P(('blk', 'red', 'sub'), None, 'grp'), parts along dimension 2
The draws below stay inside these ranges and needn't reach their ends.
There are 2 independent parts, one for each index of `grp`. The reference program is written for one: setup_inputs(seed, part) draws one part's arguments, and reference() takes and returns one part's arrays. A program takes and returns all parts, laid end to end along the dimension named above; an argument that names none is the same for every part. Nothing has to cross between parts.
All inputs are finite; a program needn't handle non-finite values.
Results may differ from the reference program's by a relative error of at most 0.03.
Values may be sent and summed in bfloat16 or wider, within the bound.
A program may use at most 128 MiB of HBM per device.

```python
import math
import jax
import jax.numpy as jnp
from jax import lax

D = 8192
E = 16384
N = 16
R = 512
KC = 4
SEQS = 128
P_SIZE = 544


def draw_tokens(key, part):
    key = jax.random.fold_in(key, 11)
    col_key = jax.random.fold_in(key, 0)
    val_key = jax.random.fold_in(key, 2)
    column_scale = 0.3 * jnp.exp(jax.random.uniform(col_key, (1, D), jnp.float32, 0.0, math.log(10.0)))
    values = jnp.clip(jax.random.normal(val_key, (SEQS, D), jnp.float32), -4.0, 4.0)
    return (values * column_scale).astype(jnp.bfloat16)


def level_of(stream_key, dims, cuts, least, high):
    loudness = 1.0
    for axis_at, blocks in cuts:
        draws = jax.random.uniform(jax.random.fold_in(jax.random.fold_in(stream_key, 6), axis_at), (blocks,), jnp.float32, least / len(cuts), high / len(cuts))
        loudness = loudness * jnp.repeat(jnp.exp(draws), dims[axis_at] // blocks).reshape((-1,) + (1,) * (len(dims) - 1 - axis_at))
    return loudness


def bell_draw(key, dims, width, most, cuts=(), kind=jnp.bfloat16):
    entries = width * jax.random.normal(key, dims, jnp.float32)
    if cuts:
        entries = entries * level_of(key, dims, cuts, -0.22, 0.18)
    return jnp.clip(entries, -most, most).astype(kind)


def setup_inputs(seed: int = 0, part: int = 0) -> dict:
    key_of = jax.random.split(jax.random.key(seed), 17)
    part_splits = jax.random.split(jax.random.fold_in(key_of[16], part), 17)
    tokens = draw_tokens(jax.random.fold_in(jax.random.fold_in(key_of[16], part), 71), part)
    input_gain = jnp.clip(1.0 + 0.1 * jax.random.normal(key_of[1], (D,), jnp.float32), 0.5, 1.5).astype(jnp.bfloat16)
    in_weight = bell_draw(key_of[2], (2, D, E), D ** -0.5, 0.0625, ((2, 16),))
    conv_weight = bell_draw(key_of[3], (KC, E), 0.5, 2.5, ((1, 16),))
    conv_bias = jnp.clip(jax.random.uniform(key_of[4], (E,), jnp.float32, -0.5, 0.5) * level_of(key_of[4], (E,), ((0, 16),), -0.4, 0.0), -0.5, 0.5).astype(jnp.bfloat16)
    param_weight = bell_draw(key_of[5], (E, P_SIZE), E ** -0.5, 0.046875, ((0, 16),))
    step_gain = jnp.clip(1.0 + 0.15 * jax.random.normal(key_of[6], (R,), jnp.float32), 0.25, 1.75).astype(jnp.bfloat16)
    entry_gain = jnp.clip(1.0 + 0.18 * jax.random.normal(key_of[7], (N,), jnp.float32), 0.099609375, 1.8984375).astype(jnp.bfloat16)
    readout_gain = jnp.clip(1.0 + 0.18 * jax.random.normal(key_of[8], (N,), jnp.float32), 0.099609375, 1.8984375).astype(jnp.bfloat16)
    step_weight = bell_draw(key_of[9], (R, E), R ** -0.5, 0.25, ((1, 16),))
    step_bias = jnp.clip(-2.0 + 2.5 * jax.random.uniform(key_of[10], (E,), jnp.float32) ** level_of(key_of[10], (E,), ((0, 16),), -0.2, 0.2), -2.0, 0.5)
    decay_log = jnp.clip(2.77 * jax.random.uniform(key_of[11], (N, E), jnp.float32) ** level_of(key_of[11], (N, E), ((1, 16),), -0.2, 0.2), 0.0, 2.77)
    skip_gain = jnp.clip(0.5 + 1.0 * jax.random.uniform(key_of[12], (E,), jnp.float32) ** level_of(key_of[12], (E,), ((0, 16),), -0.2, 0.2), 0.5, 1.5)
    out_weight = bell_draw(key_of[13], (E, D), E ** -0.5, 0.046875, ((0, 8), (1, 2)))
    conv_state = bell_draw(part_splits[14], (KC - 1, E, SEQS), 1.0, 5.0, ((1, 16),))
    scan_state = bell_draw(part_splits[15], (E, N, SEQS), 1.0, 5.0, ((0, 16),))
    return dict(tokens=tokens, input_gain=input_gain, in_weight=in_weight, conv_weight=conv_weight, conv_bias=conv_bias, param_weight=param_weight, step_gain=step_gain, entry_gain=entry_gain, readout_gain=readout_gain, step_weight=step_weight, step_bias=step_bias, decay_log=decay_log, skip_gain=skip_gain, out_weight=out_weight, conv_state=conv_state, scan_state=scan_state)


def matmul(left, right):
    return jnp.dot(left.astype(jnp.float32), right.astype(jnp.float32), precision=lax.Precision.HIGHEST)

def normalize(matrix, gain):
    return matrix * lax.rsqrt(lax.optimization_barrier(jnp.mean(matrix * matrix, axis=0, keepdims=True)) + 1e-06) * gain.astype(jnp.float32)[:, None]

def reference(tokens, input_gain, in_weight, conv_weight, conv_bias, param_weight, step_gain, entry_gain, readout_gain, step_weight, step_bias, decay_log, skip_gain, out_weight, conv_state, scan_state):
    wide = tokens.astype(jnp.float32)
    normed = (wide * lax.rsqrt(lax.optimization_barrier(jnp.mean(wide * wide, axis=1, keepdims=True)) + 1e-06) * input_gain.astype(jnp.float32)[None, :]).astype(jnp.bfloat16)
    branch = matmul(normed, in_weight[0]).T.astype(jnp.bfloat16)
    gating = matmul(normed, in_weight[1]).T.astype(jnp.bfloat16)
    window = jnp.concatenate([conv_state, branch[None]], axis=0)
    new_conv = window[1:]
    convolved = lax.optimization_barrier(jnp.sum(window.astype(jnp.float32) * conv_weight.astype(jnp.float32)[:, :, None], axis=0)) + conv_bias.astype(jnp.float32)[:, None]
    activated = jax.nn.silu(convolved).astype(jnp.bfloat16)
    params = matmul(param_weight.T, activated)
    step_low = normalize(params[:R], step_gain).astype(jnp.bfloat16)
    entry = normalize(params[R:R + N], entry_gain).astype(jnp.bfloat16)
    readout = normalize(params[R + N:], readout_gain).astype(jnp.bfloat16)
    step = jax.nn.softplus(matmul(step_weight.T, step_low) + step_bias[:, None])
    active_wide = activated.astype(jnp.float32)
    rates = (-jnp.exp(decay_log)).T
    state = jnp.exp(step[:, None, :] * rates[:, :, None]) * scan_state.astype(jnp.float32)
    state = state + (step * active_wide)[:, None, :] * entry.astype(jnp.float32)[None, :, :]
    gated = lax.optimization_barrier(jnp.sum(state * readout.astype(jnp.float32)[None, :, :], axis=1)) + skip_gain[:, None] * active_wide
    gated = (gated * jax.nn.silu(gating.astype(jnp.float32))).astype(jnp.bfloat16)
    output = matmul(gated.T, out_weight)
    mixed = (wide + output).astype(jnp.bfloat16)
    return (mixed, new_conv, state.astype(jnp.bfloat16))
```

```python
import jax
import jax.numpy as jnp
from jax import lax
from jax.sharding import PartitionSpec as P


def contract(left, right, dims):
    return lax.dot_general(
        left,
        right,
        (dims, ((), ())),
        preferred_element_type=jnp.float32,
    )


def normalize(matrix, gain):
    return (
        matrix
        * lax.rsqrt(jnp.mean(matrix * matrix, axis=0, keepdims=True) + 1e-06)
        * gain.astype(jnp.float32)[:, None]
    )


def prenorm(rows_in, input_gain):
    wide = rows_in.astype(jnp.float32)
    scaled = wide * lax.rsqrt(jnp.mean(wide * wide, axis=1, keepdims=True) + 1e-06)
    return (scaled * input_gain.astype(jnp.float32)[None, :]).astype(jnp.bfloat16)


def split_params(summed, step_gain, entry_gain, readout_gain):
    width_low = step_gain.shape[0]
    width_state = entry_gain.shape[0]
    step_low = normalize(summed[:width_low], step_gain).astype(jnp.bfloat16)
    entry = normalize(summed[width_low : width_low + width_state], entry_gain).astype(jnp.bfloat16)
    readout = normalize(summed[width_low + width_state :], readout_gain).astype(jnp.bfloat16)
    return (step_low, entry, readout)


def body(
    tokens,
    input_gain,
    in_weight,
    conv_weight,
    conv_bias,
    param_weight,
    step_gain,
    entry_gain,
    readout_gain,
    step_weight,
    step_bias,
    decay_log,
    skip_gain,
    out_weight,
    conv_state,
    scan_state,
):
    all_rows = lax.all_gather(tokens, "blk", axis=0, tiled=True)
    full_rows = lax.all_gather(all_rows, ("red", "sub"), axis=1, tiled=True)
    row_piece = prenorm(full_rows, input_gain)
    first = contract(in_weight[0], row_piece, ((0,), (1,)))
    second = contract(in_weight[1], row_piece, ((0,), (1,)))
    projected = jnp.stack([first, second], axis=0)
    branch = projected[0].astype(jnp.bfloat16)
    gating = projected[1].astype(jnp.bfloat16)
    window = jnp.concatenate([conv_state, branch[None]], axis=0)
    new_conv = window[1:]
    convolved = (
        jnp.sum(window.astype(jnp.float32) * conv_weight.astype(jnp.float32)[:, :, None], axis=0)
        + conv_bias.astype(jnp.float32)[:, None]
    )
    activated = jax.nn.silu(convolved).astype(jnp.bfloat16)
    param_terms = contract(param_weight, activated, ((0,), (0,)))
    summed = lax.psum(param_terms, ("blk", "red", "sub"))
    step_low, entry, readout = split_params(summed, step_gain, entry_gain, readout_gain)
    step = jax.nn.softplus(contract(step_weight, step_low, ((0,), (0,))) + step_bias[:, None])
    active_wide = activated.astype(jnp.float32)
    rates = (-jnp.exp(decay_log)).T
    state = jnp.exp(step[:, None, :] * rates[:, :, None]) * scan_state.astype(jnp.float32)
    state = state + (step * active_wide)[:, None, :] * entry.astype(jnp.float32)[None, :, :]
    gated = (
        jnp.sum(state * readout.astype(jnp.float32)[None, :, :], axis=1)
        + skip_gain[:, None] * active_wide
    )
    gated = (gated * jax.nn.silu(gating.astype(jnp.float32))).astype(jnp.bfloat16)
    gathered = lax.all_gather(gated, ("red", "sub"), axis=0, tiled=True)
    output = lax.psum_scatter(
        contract(gathered, out_weight, ((0,), (0,))).astype(jnp.bfloat16),
        "blk",
        scatter_dimension=0,
        tiled=True,
    ).astype(jnp.float32)
    mixed = (tokens.astype(jnp.float32) + output).astype(jnp.bfloat16)
    return (mixed, new_conv, state.astype(jnp.bfloat16))


def solution(mesh):
    placed = (
        P(("grp", "blk"), ("red", "sub")),
        P(),
        P(None, None, ("blk", "red", "sub")),
        P(None, ("blk", "red", "sub")),
        P(("blk", "red", "sub")),
        P(("blk", "red", "sub"), None),
        P(),
        P(),
        P(),
        P(None, ("blk", "red", "sub")),
        P(("blk", "red", "sub")),
        P(None, ("blk", "red", "sub")),
        P(("blk", "red", "sub")),
        P("blk", ("red", "sub")),
        P(None, ("blk", "red", "sub"), "grp"),
        P(("blk", "red", "sub"), None, "grp"),
    )
    return jax.shard_map(
        body,
        mesh=mesh,
        in_specs=placed,
        out_specs=(
            P(("grp", "blk"), ("red", "sub")),
            P(None, ("blk", "red", "sub"), "grp"),
            P(("blk", "red", "sub"), None, "grp"),
        ),
        check_vma=False,
    )
```

```python
import functools
import jax
import jax.numpy as jnp
from jax import lax
from jax.experimental import pallas as pl
from jax.experimental.pallas import tpu as pltpu
from jax.sharding import PartitionSpec as P


def contract(left, right, dims):
    return lax.dot_general(
        left,
        right,
        (dims, ((), ())),
        preferred_element_type=jnp.float32,
    )


def normalize(matrix, gain):
    return (
        matrix
        * lax.rsqrt(jnp.mean(matrix * matrix, axis=0, keepdims=True) + 1e-06)
        * gain.astype(jnp.float32)[:, None]
    )


def prenorm(rows_in, input_gain):
    wide = rows_in.astype(jnp.float32)
    scaled = wide * lax.rsqrt(jnp.mean(wide * wide, axis=1, keepdims=True) + 1e-06)
    return (scaled * input_gain.astype(jnp.float32)[None, :]).astype(jnp.bfloat16)


def split_params(summed, step_gain, entry_gain, readout_gain):
    width_low = step_gain.shape[0]
    width_state = entry_gain.shape[0]
    step_low = normalize(summed[:width_low], step_gain).astype(jnp.bfloat16)
    entry = normalize(summed[width_low : width_low + width_state], entry_gain).astype(jnp.bfloat16)
    readout = normalize(summed[width_low + width_state :], readout_gain).astype(jnp.bfloat16)
    return (step_low, entry, readout)


def body(
    tokens,
    input_gain,
    in_weight,
    conv_weight,
    conv_bias,
    param_weight,
    step_gain,
    entry_gain,
    readout_gain,
    step_weight,
    step_bias,
    decay_log,
    skip_gain,
    out_weight,
    conv_state,
    scan_state,
):
    all_rows = lax.all_gather(tokens, "blk", axis=0, tiled=True)
    full_rows = lax.all_gather(all_rows, ("red", "sub"), axis=1, tiled=True)
    row_piece = prenorm(full_rows, input_gain)
    first = contract(in_weight[0], row_piece, ((0,), (1,)))
    second = contract(in_weight[1], row_piece, ((0,), (1,)))
    projected = jnp.stack([first, second], axis=0)
    branch = projected[0].astype(jnp.bfloat16)
    gating = projected[1].astype(jnp.bfloat16)
    window = jnp.concatenate([conv_state, branch[None]], axis=0)
    new_conv = window[1:]
    convolved = (
        jnp.sum(window.astype(jnp.float32) * conv_weight.astype(jnp.float32)[:, :, None], axis=0)
        + conv_bias.astype(jnp.float32)[:, None]
    )
    activated = jax.nn.silu(convolved).astype(jnp.bfloat16)
    param_terms = contract(param_weight, activated, ((0,), (0,)))
    summed = lax.psum(param_terms, ("blk", "red", "sub"))
    step_low, entry, readout = split_params(summed, step_gain, entry_gain, readout_gain)
    step = jax.nn.softplus(contract(step_weight, step_low, ((0,), (0,))) + step_bias[:, None])
    active_wide = activated.astype(jnp.float32)
    rates = (-jnp.exp(decay_log)).T
    state = jnp.exp(step[:, None, :] * rates[:, :, None]) * scan_state.astype(jnp.float32)
    state = state + (step * active_wide)[:, None, :] * entry.astype(jnp.float32)[None, :, :]
    gated = (
        jnp.sum(state * readout.astype(jnp.float32)[None, :, :], axis=1)
        + skip_gain[:, None] * active_wide
    )
    gated = (gated * jax.nn.silu(gating.astype(jnp.float32))).astype(jnp.bfloat16)
    gathered = lax.all_gather(gated, ("red", "sub"), axis=0, tiled=True)
    output = lax.psum_scatter(
        contract(gathered, out_weight, ((0,), (0,))).astype(jnp.bfloat16),
        "blk",
        scatter_dimension=0,
        tiled=True,
    ).astype(jnp.float32)
    mixed = (tokens.astype(jnp.float32) + output).astype(jnp.bfloat16)
    return (mixed, new_conv, state.astype(jnp.bfloat16))


MESH = pl.DeviceIdType.MESH
F32 = jnp.float32
BF16 = jnp.bfloat16
LANES = 128
HALF = 384
RING = 6
PARTS = 4


def silu(v):
    return v / (1.0 + jnp.exp(-v))


def softplus(v):
    return jnp.maximum(v, 0.0) + jnp.log1p(jnp.exp(-jnp.abs(v)))


def kernel(
    blocks,
    tokens,
    gain,
    in_w,
    conv_w,
    conv_b,
    par_w,
    step_gain,
    entry_gain,
    read_gain,
    step_w,
    step_b,
    decay_log,
    skip,
    out_w,
    conv_in,
    scan_in,
    mixed,
    conv_out,
    scan_out,
    tok,
    scaled,
    squares,
    iw,
    acc,
    pw,
    sw,
    ow,
    conv,
    branch,
    scan,
    small,
    small_t,
    rates,
    act,
    act_t,
    gate,
    step,
    drive,
    pp,
    prv,
    pall,
    low,
    inout,
    dot_out,
    heads,
    part,
    sib,
    mine,
    far,
    mix,
    load_sem,
    iw_sem,
    store_sem,
    scan_sem,
    tok_recv,
    tok_z,
    tok_x,
    tok_sib,
    par_send,
    par_recv,
    all_send,
    all_recv,
    head_send,
    head_recv,
    sib_send,
    sib_recv,
    far_send,
    far_recv,
):
    g = lax.axis_index("grp")
    b = lax.axis_index("blk")
    x = lax.axis_index("red")
    z = b // 2
    c = b % 2
    nz = blocks // 2
    me = b * 2 + x
    total = blocks * 2
    rows = tokens.shape[0]
    wide = tokens.shape[1]
    seqs = rows * blocks
    chan = act.shape[0]
    kc = wide // PARTS
    nblk = chan // LANES
    twin = (g, b + 1 - 2 * c, x, 0)
    peer = (g, b, 1 - x, 0)

    def load(src, dst, at):
        return pltpu.make_async_copy(src, dst, load_sem.at[at])

    def weight(t):
        h, j = t // PARTS, t % PARTS
        start = ((x + h) % 2) * wide + j * kc
        return pltpu.make_async_copy(
            in_w.at[:, pl.ds(pl.multiple_of(start, kc), kc), :],
            iw.at[t % RING],
            iw_sem.at[t % RING],
        )

    def block_rows(at):
        return pl.ds(pl.multiple_of(at * rows, rows), rows)

    first = load(tokens, tok.at[x, block_rows(b)], 0)
    first.start()
    for t in range(RING):
        weight(t).start()
    get_conv = load(conv_in, conv, 1)
    get_pw = load(par_w, pw, 2)
    get_sw = load(step_w, sw, 3)
    get_scan = load(scan_in, scan, 4)
    get_ow = load(out_w, ow, 5)
    get_conv.start()
    get_pw.start()
    get_sw.start()

    barrier = pltpu.get_barrier_semaphore()

    def partner(k):
        idx = lax.rem(me + k, total)
        return (g, idx // 2, idx % 2, 0), idx

    def greet(k, carry):
        pl.semaphore_signal(barrier, inc=1, device_id=partner(k)[0], device_id_type=MESH)
        return carry

    lax.fori_loop(1, total, greet, 0)
    pl.semaphore_wait(barrier, total - 1)

    def send(src, dst, ssem, rsem, where):
        return pltpu.make_async_remote_copy(
            src_ref=src, dst_ref=dst, send_sem=ssem, recv_sem=rsem, device_id=where, device_id_type=MESH
        )

    def tok_copy(half, blk, ssem, where):
        ref = tok.at[half, block_rows(blk)]
        return send(ref, ref, ssem, tok_recv.at[half, blk], where)

    def to_z(k):
        z_to = lax.rem(z + k, nz)
        return tok_copy(x, b, tok_z.at[k], (g, z_to * 2 + c, x, 0))

    def to_peer(k):
        blk = lax.rem(z + k, nz) * 2 + c
        return tok_copy(x, blk, tok_x.at[k], peer)

    def to_twin(h, k):
        blk = lax.rem(z + k, nz) * 2 + c
        return tok_copy((x + h) % 2, blk, tok_sib.at[h, k], twin)

    def got(half, blk):
        ref = tok.at[half, block_rows(blk)]
        send(ref, ref, tok_z.at[0], tok_recv.at[half, blk], peer).wait_recv()

    first.wait()
    to_peer(0).start()
    for k in range(1, nz):
        to_z(k).start()
    to_twin(0, 0).start()

    small[...] = jnp.zeros_like(small)
    small[0:4, :] = conv_w[...].astype(F32)
    small[4:5, :] = conv_b[...].astype(F32)
    small[5:6, :] = step_b[...]
    small[6:7, :] = skip[...]
    rates[...] = -jnp.exp(decay_log[...])

    def flip_small(i, carry):
        at = pl.ds(pl.multiple_of(i * LANES, LANES), LANES)
        small_t[at, :] = small[:, at].T
        return carry

    lax.fori_loop(0, nblk, flip_small, 0)
    squares[...] = jnp.zeros_like(squares)
    acc[...] = jnp.zeros_like(acc)
    pp[...] = jnp.zeros_like(pp)

    for k in range(1, nz):
        got(x, lax.rem(z + k, nz) * 2 + c)
        to_peer(k).start()
        to_twin(0, k).start()

    for h in range(2):
        half = (x + h) % 2
        if h == 1:
            for k in range(nz):
                got(half, lax.rem(z + k, nz) * 2 + c)
                to_twin(1, k).start()
        for k in range(nz):
            got(half, lax.rem(z + k, nz) * 2 + 1 - c)

        def scale(j, carry):
            at = pl.ds(pl.multiple_of(j * LANES, LANES), LANES)
            col = pl.ds(pl.multiple_of(half * wide + j * LANES, LANES), LANES)
            v = tok[half, :, at].astype(F32)
            squares[...] += v * v
            scaled[:, at] = (v * gain[:, col].astype(F32)).astype(BF16)
            return carry

        lax.fori_loop(0, wide // LANES, scale, 0)

        def project(j, carry):
            t = h * PARTS + j
            weight(t).wait()
            lhs = scaled[:, pl.ds(pl.multiple_of(j * kc, kc), kc)]
            slot = t % RING
            for w in range(2):
                acc[w] += jnp.dot(lhs, iw[slot, w], preferred_element_type=F32)

            @pl.when(t + RING < 2 * PARTS)
            def _():
                weight(t + RING).start()

            return carry

        lax.fori_loop(0, PARTS, project, 0)
        if h == 0:
            get_scan.start()
            get_ow.start()

    inv = lax.rsqrt(jnp.sum(squares[...], axis=1, keepdims=True) / (2.0 * wide) + 1e-06)
    get_conv.wait()

    def convolve(i, carry):
        at = pl.ds(pl.multiple_of(i * LANES, LANES), LANES)
        br = (acc[0, :, at] * inv).T.astype(BF16)
        branch[at, :] = br
        cols = small_t[at, :]
        v = br.astype(F32) * cols[:, 3:4]
        for k in range(3):
            v += conv[k, at, :].astype(F32) * cols[:, k : k + 1]
        a = silu(v + cols[:, 4:5]).astype(BF16).astype(F32)
        act[at, :] = a
        act_t[:, at] = a.T.astype(BF16)
        gt = (acc[1, :, at] * inv).T.astype(BF16).astype(F32)
        gate[at, :] = silu(gt)
        return carry

    lax.fori_loop(0, nblk, convolve, 0)
    put_conv = pltpu.make_async_copy(conv.at[pl.ds(1, 2)], conv_out.at[pl.ds(0, 2)], store_sem.at[0])
    put_branch = pltpu.make_async_copy(branch, conv_out.at[2], store_sem.at[1])
    put_conv.start()
    put_branch.start()

    get_pw.wait()
    width = pw.shape[1]
    terms = jnp.dot(act_t[...], pw[...], preferred_element_type=F32).astype(BF16)
    pp[0] = terms[:, 0:HALF].reshape(blocks, rows, HALF)
    dot_out[...] = jnp.zeros_like(dot_out)
    dot_out[:, 0 : width - HALF] = terms[:, HALF:width]
    pp[1] = dot_out[...].reshape(blocks, rows, HALF)

    def par_copy(k):
        where, idx = partner(k)
        return send(pp.at[idx % 2, idx // 2], prv.at[me], par_send.at[k], par_recv.at[me], where)

    def all_copy(k):
        where, idx = partner(k)
        ref = pall.at[x, b]
        return send(ref, ref, all_send.at[k], all_recv.at[me], where)

    def start_par(k, carry):
        par_copy(k).start()
        return carry

    lax.fori_loop(1, total, start_par, 0)

    def take_par(k, summed):
        where, idx = partner(k)
        send(prv.at[idx], prv.at[idx], par_send.at[0], par_recv.at[idx], where).wait_recv()
        return summed + prv[idx].astype(F32)

    summed = lax.fori_loop(1, total, take_par, pp[x, b].astype(F32))
    pall[x, b] = summed.astype(BF16)

    def start_all(k, carry):
        all_copy(k).start()
        return carry

    lax.fori_loop(1, total, start_all, 0)
    get_sw.wait()
    get_scan.wait()

    def take_all(k, carry):
        where, idx = partner(k)
        ref = pall.at[idx % 2, idx // 2]
        send(ref, ref, all_send.at[0], all_recv.at[idx], where).wait_recv()
        return carry

    lax.fori_loop(1, total, take_all, 0)

    one = pall[0].astype(F32).reshape(seqs, HALF)
    two = pall[1].astype(F32).reshape(seqs, HALF)
    rank = step_gain.shape[1]
    extra = two[:, 0 : rank - HALF]
    norm = lax.rsqrt(
        (jnp.sum(one * one, axis=1, keepdims=True) + jnp.sum(extra * extra, axis=1, keepdims=True)) / rank
        + 1e-06
    )
    gains = step_gain[...].astype(F32)
    low[:, 0:HALF] = (one * norm * gains[:, 0:HALF]).astype(BF16)
    low[:, HALF:rank] = (extra * norm * gains[:, HALF:rank]).astype(BF16)
    flipped = two[:, rank - HALF : rank - HALF + LANES].T
    states = entry_gain.shape[0]

    def short(v, weights):
        v = v * lax.rsqrt(jnp.mean(v * v, axis=0, keepdims=True) + 1e-06) * weights[...].astype(F32)
        return v.astype(BF16).astype(F32)

    inout[0] = short(flipped[0:states], entry_gain)
    inout[1] = short(flipped[states : 2 * states], read_gain)

    def head_copy(i):
        at = pl.ds(pl.multiple_of(x * chan + i * LANES, LANES), LANES)
        ref = heads.at[:, at]
        return send(ref, ref, head_send.at[i], head_recv.at[i], peer)

    def head_got(i):
        at = pl.ds(pl.multiple_of((1 - x) * chan + i * LANES, LANES), LANES)
        ref = heads.at[:, at]
        send(ref, ref, head_send.at[i], head_recv.at[i], peer).wait_recv()

    def put_scan(i):
        at = pl.ds(pl.multiple_of(i * LANES, LANES), LANES)
        return pltpu.make_async_copy(scan.at[at], scan_out.at[at], scan_sem.at[i])

    def advance(i, carry):
        base = pl.multiple_of(i * LANES, LANES)
        at = pl.ds(base, LANES)
        cols = small_t[at, :]
        raw = jnp.dot(low[...], sw[:, at], preferred_element_type=F32).T
        st = softplus(raw + cols[:, 5:6])
        step[...] = st
        drive[...] = st * act[at, :]
        decay = rates[:, at]

        def group(q, inner):
            rolled = pltpu.roll(decay, LANES - q * 8, 1)
            entry = inout[0]
            readout = inout[1]
            for j in range(8):
                e = q * 8 + j
                fade = jnp.exp(step[pl.ds(e, 1), :] * rolled[:, j : j + 1])
                state = fade * scan[base + e].astype(F32) + drive[pl.ds(e, 1), :] * entry
                scan[base + e] = state.astype(BF16)
                step[pl.ds(e, 1), :] = jnp.sum(state * readout, axis=0, keepdims=True)
            return inner

        lax.fori_loop(0, LANES // 8, group, 0)
        put_scan(i).start()
        out = (step[...] + cols[:, 6:7] * act[at, :]) * gate[at, :]
        heads[:, pl.ds(pl.multiple_of(x * chan + i * LANES, LANES), LANES)] = out.T.astype(BF16)
        head_copy(i).start()
        return carry

    lax.fori_loop(0, nblk, advance, 0)
    get_ow.wait()

    def wait_heads(i, carry):
        head_got(i)
        return carry

    lax.fori_loop(0, nblk, wait_heads, 0)

    def sib_copy(n):
        return send(part.at[n, :, 1 - c], sib.at[n], sib_send.at[n], sib_recv.at[n], twin)

    def far_copy(n, k):
        z_to = lax.rem(z + k, nz)
        return send(
            mine.at[n, z_to], far.at[n, k], far_send.at[n, k], far_recv.at[n, k], (g, z_to * 2 + c, x, 0)
        )

    for n in range(PARTS + 1):
        if n < PARTS:
            p = jnp.dot(heads[...], ow[:, n * kc : (n + 1) * kc], preferred_element_type=F32)
            part[n] = p.astype(BF16).reshape(nz, 2, rows, kc)
            sib_copy(n).start()
        if n > 0:
            m = n - 1
            sib_copy(m).wait_recv()
            mine[m] = (part[m, :, c].astype(F32) + sib[m].astype(F32)).astype(BF16)
            for k in range(1, nz):
                far_copy(m, k).start()

    for n in range(PARTS):
        v = mine[n, z].astype(F32)
        for k in range(1, nz):
            far_copy(n, k).wait_recv()
            v += far[n, k].astype(F32)
        at = slice(n * kc, (n + 1) * kc)
        own = tok[x, block_rows(b), at].astype(F32)
        mix[:, at] = (own + v).astype(BF16)
    put_mix = pltpu.make_async_copy(mix, mixed, store_sem.at[2])
    put_mix.start()

    for k in range(nz):
        to_peer(k).wait_send()
        to_twin(0, k).wait_send()
        to_twin(1, k).wait_send()
    for k in range(1, nz):
        to_z(k).wait_send()

    def drain(k, carry):
        par_copy(k).wait_send()
        all_copy(k).wait_send()
        return carry

    lax.fori_loop(1, total, drain, 0)

    def drain_blocks(i, carry):
        head_copy(i).wait_send()
        put_scan(i).wait()
        return carry

    lax.fori_loop(0, nblk, drain_blocks, 0)
    for n in range(PARTS):
        sib_copy(n).wait_send()
        for k in range(1, nz):
            far_copy(n, k).wait_send()
    put_conv.wait()
    put_branch.wait()
    put_mix.wait()


def fused(
    blocks,
    tokens,
    input_gain,
    in_weight,
    conv_weight,
    conv_bias,
    param_weight,
    step_gain,
    entry_gain,
    readout_gain,
    step_weight,
    step_bias,
    decay_log,
    skip_gain,
    out_weight,
    conv_state,
    scan_state,
):
    rows, wide = tokens.shape
    seqs = rows * blocks
    chan = in_weight.shape[2]
    rank = step_gain.shape[0]
    states = entry_gain.shape[0]
    nz = blocks // 2
    kc = wide // PARTS
    nblk = chan // LANES
    total = 2 * blocks
    vm = pl.BlockSpec(memory_space=pltpu.VMEM)
    hbm = pl.BlockSpec(memory_space=pl.ANY)
    dma = pltpu.SemaphoreType.DMA
    v = pltpu.VMEM
    scratch = [
        v((2, seqs, wide), BF16),
        v((seqs, wide), BF16),
        v((seqs, LANES), F32),
        v((RING, 2, kc, chan), BF16),
        v((2, seqs, chan), F32),
        v(param_weight.shape, BF16),
        v(step_weight.shape, BF16),
        v(out_weight.shape, BF16),
        v(conv_state.shape, BF16),
        v((chan, seqs), BF16),
        v(scan_state.shape, BF16),
        v((LANES, chan), F32),
        v((chan, LANES), F32),
        v((states, chan), F32),
        v((chan, seqs), F32),
        v((seqs, chan), BF16),
        v((chan, seqs), F32),
        v((LANES, seqs), F32),
        v((LANES, seqs), F32),
        v((2, blocks, rows, HALF), BF16),
        v((total, rows, HALF), BF16),
        v((2, blocks, rows, HALF), BF16),
        v((seqs, rank), BF16),
        v((2, states, seqs), F32),
        v((seqs, HALF), BF16),
        v((seqs, 2 * chan), BF16),
        v((PARTS, nz, 2, rows, kc), BF16),
        v((PARTS, nz, rows, kc), BF16),
        v((PARTS, nz, rows, kc), BF16),
        v((PARTS, nz, rows, kc), BF16),
        v((rows, wide), BF16),
        dma((6,)),
        dma((RING,)),
        dma((3,)),
        dma((nblk,)),
        dma((2, blocks)),
        dma((nz,)),
        dma((nz,)),
        dma((2, nz)),
        dma((total,)),
        dma((total,)),
        dma((total,)),
        dma((total,)),
        dma((nblk,)),
        dma((nblk,)),
        dma((PARTS,)),
        dma((PARTS,)),
        dma((PARTS, nz)),
        dma((PARTS, nz)),
    ]
    return pl.pallas_call(
        functools.partial(kernel, blocks),
        out_shape=(
            jax.ShapeDtypeStruct(tokens.shape, BF16),
            jax.ShapeDtypeStruct(conv_state.shape, BF16),
            jax.ShapeDtypeStruct(scan_state.shape, BF16),
        ),
        in_specs=[hbm, vm, hbm, vm, vm, hbm, vm, vm, vm, hbm, vm, vm, vm, hbm, hbm, hbm],
        out_specs=(hbm, hbm, hbm),
        scratch_shapes=scratch,
        compiler_params=pltpu.CompilerParams(
            collective_id=0, has_side_effects=True, vmem_limit_bytes=62 * 1024 * 1024
        ),
    )(
        tokens,
        input_gain[None, :],
        in_weight,
        conv_weight,
        conv_bias[None, :],
        param_weight,
        step_gain[None, :],
        entry_gain[:, None],
        readout_gain[:, None],
        step_weight,
        step_bias[None, :],
        decay_log,
        skip_gain[None, :],
        out_weight,
        conv_state,
        scan_state,
    )


def fits(mesh, tokens, in_weight, step_gain, entry_gain, conv_weight):
    rows, wide = tokens.shape
    width = step_gain.shape[0] + 2 * entry_gain.shape[0]
    return (
        mesh.shape["sub"] == 1
        and mesh.shape["red"] == 2
        and mesh.shape["blk"] % 2 == 0
        and rows == 16
        and rows * mesh.shape["blk"] == LANES
        and in_weight.shape[2] % LANES == 0
        and wide % (PARTS * LANES) == 0
        and HALF < step_gain.shape[0] == HALF + LANES
        and width <= 2 * HALF
        and entry_gain.shape[0] == 16
        and conv_weight.shape[0] == 4
    )


def solution(mesh):
    def chosen(*args):
        if fits(mesh, args[0], args[2], args[6], args[7], args[3]):
            return fused(mesh.shape["blk"], *args)
        return body(*args)

    placed = (
        P(("grp", "blk"), ("red", "sub")),
        P(),
        P(None, None, ("blk", "red", "sub")),
        P(None, ("blk", "red", "sub")),
        P(("blk", "red", "sub")),
        P(("blk", "red", "sub"), None),
        P(),
        P(),
        P(),
        P(None, ("blk", "red", "sub")),
        P(("blk", "red", "sub")),
        P(None, ("blk", "red", "sub")),
        P(("blk", "red", "sub")),
        P("blk", ("red", "sub")),
        P(None, ("blk", "red", "sub"), "grp"),
        P(("blk", "red", "sub"), None, "grp"),
    )
    return jax.shard_map(
        chosen,
        mesh=mesh,
        in_specs=placed,
        out_specs=(
            P(("grp", "blk"), ("red", "sub")),
            P(None, ("blk", "red", "sub"), "grp"),
            P(("blk", "red", "sub"), None, "grp"),
        ),
        check_vma=False,
    )
```

```python
import functools
import jax
import jax.numpy as jnp
from jax import lax
from jax.experimental import pallas as pl
from jax.experimental.pallas import tpu as pltpu
from jax.sharding import PartitionSpec as P


def contract(left, right, dims):
    return lax.dot_general(
        left,
        right,
        (dims, ((), ())),
        preferred_element_type=jnp.float32,
    )


def normalize(matrix, gain):
    return (
        matrix
        * lax.rsqrt(jnp.mean(matrix * matrix, axis=0, keepdims=True) + 1e-06)
        * gain.astype(jnp.float32)[:, None]
    )


def prenorm(rows_in, input_gain):
    wide = rows_in.astype(jnp.float32)
    scaled = wide * lax.rsqrt(jnp.mean(wide * wide, axis=1, keepdims=True) + 1e-06)
    return (scaled * input_gain.astype(jnp.float32)[None, :]).astype(jnp.bfloat16)


def split_params(summed, step_gain, entry_gain, readout_gain):
    width_low = step_gain.shape[0]
    width_state = entry_gain.shape[0]
    step_low = normalize(summed[:width_low], step_gain).astype(jnp.bfloat16)
    entry = normalize(summed[width_low : width_low + width_state], entry_gain).astype(jnp.bfloat16)
    readout = normalize(summed[width_low + width_state :], readout_gain).astype(jnp.bfloat16)
    return (step_low, entry, readout)


def body(
    tokens,
    input_gain,
    in_weight,
    conv_weight,
    conv_bias,
    param_weight,
    step_gain,
    entry_gain,
    readout_gain,
    step_weight,
    step_bias,
    decay_log,
    skip_gain,
    out_weight,
    conv_state,
    scan_state,
):
    all_rows = lax.all_gather(tokens, "blk", axis=0, tiled=True)
    full_rows = lax.all_gather(all_rows, ("red", "sub"), axis=1, tiled=True)
    row_piece = prenorm(full_rows, input_gain)
    first = contract(in_weight[0], row_piece, ((0,), (1,)))
    second = contract(in_weight[1], row_piece, ((0,), (1,)))
    projected = jnp.stack([first, second], axis=0)
    branch = projected[0].astype(jnp.bfloat16)
    gating = projected[1].astype(jnp.bfloat16)
    window = jnp.concatenate([conv_state, branch[None]], axis=0)
    new_conv = window[1:]
    convolved = (
        jnp.sum(window.astype(jnp.float32) * conv_weight.astype(jnp.float32)[:, :, None], axis=0)
        + conv_bias.astype(jnp.float32)[:, None]
    )
    activated = jax.nn.silu(convolved).astype(jnp.bfloat16)
    param_terms = contract(param_weight, activated, ((0,), (0,)))
    summed = lax.psum(param_terms, ("blk", "red", "sub"))
    step_low, entry, readout = split_params(summed, step_gain, entry_gain, readout_gain)
    step = jax.nn.softplus(contract(step_weight, step_low, ((0,), (0,))) + step_bias[:, None])
    active_wide = activated.astype(jnp.float32)
    rates = (-jnp.exp(decay_log)).T
    state = jnp.exp(step[:, None, :] * rates[:, :, None]) * scan_state.astype(jnp.float32)
    state = state + (step * active_wide)[:, None, :] * entry.astype(jnp.float32)[None, :, :]
    gated = (
        jnp.sum(state * readout.astype(jnp.float32)[None, :, :], axis=1)
        + skip_gain[:, None] * active_wide
    )
    gated = (gated * jax.nn.silu(gating.astype(jnp.float32))).astype(jnp.bfloat16)
    gathered = lax.all_gather(gated, ("red", "sub"), axis=0, tiled=True)
    output = lax.psum_scatter(
        contract(gathered, out_weight, ((0,), (0,))).astype(jnp.bfloat16),
        "blk",
        scatter_dimension=0,
        tiled=True,
    ).astype(jnp.float32)
    mixed = (tokens.astype(jnp.float32) + output).astype(jnp.bfloat16)
    return (mixed, new_conv, state.astype(jnp.bfloat16))


MESH = pl.DeviceIdType.MESH
F32 = jnp.float32
BF16 = jnp.bfloat16
LANES = 128
HALF = 384
RING = 6
PARTS = 4


def silu(v):
    return v / (1.0 + jnp.exp(-v))


def softplus(v):
    return jnp.maximum(v, 0.0) + jnp.log1p(jnp.exp(-jnp.abs(v)))


def kernel(
    blocks,
    tokens,
    packed,
    in_w,
    par_w,
    step_w,
    decay_log,
    out_w,
    conv_in,
    scan_in,
    mixed,
    conv_out,
    scan_out,
    tok,
    scaled,
    squares,
    iw,
    acc,
    pw,
    sw,
    ow,
    conv,
    branch,
    scan,
    gain_row,
    small,
    small_t,
    rates,
    act,
    act_t,
    gate,
    step,
    drive,
    pp,
    prv,
    pall,
    low,
    inout,
    dot_out,
    heads,
    part,
    sib,
    mine,
    far,
    mix,
    load_sem,
    iw_sem,
    store_sem,
    scan_sem,
    tok_recv,
    tok_z,
    tok_x,
    tok_sib,
    par_send,
    par_recv,
    all_send,
    all_recv,
    head_send,
    head_recv,
    sib_send,
    sib_recv,
    far_send,
    far_recv,
):
    g = lax.axis_index("grp")
    b = lax.axis_index("blk")
    x = lax.axis_index("red")
    z = b // 2
    c = b % 2
    nz = blocks // 2
    me = b * 2 + x
    total = blocks * 2
    rows = tokens.shape[0]
    wide = tokens.shape[1]
    seqs = rows * blocks
    chan = act.shape[0]
    kc = wide // PARTS
    nblk = chan // LANES
    twin = (g, b + 1 - 2 * c, x, 0)
    peer = (g, b, 1 - x, 0)

    def load(src, dst, at):
        return pltpu.make_async_copy(src, dst, load_sem.at[at])

    def weight(t):
        h, j = t // PARTS, t % PARTS
        start = ((x + h) % 2) * wide + j * kc
        return pltpu.make_async_copy(
            in_w.at[:, pl.ds(pl.multiple_of(start, kc), kc), :],
            iw.at[t % RING],
            iw_sem.at[t % RING],
        )

    def block_rows(at):
        return pl.ds(pl.multiple_of(at * rows, rows), rows)

    first = load(tokens, tok.at[x, block_rows(b)], 0)
    first.start()
    for t in range(RING):
        weight(t).start()
    get_conv = load(conv_in, conv, 1)
    get_pw = load(par_w, pw, 2)
    get_sw = load(step_w, sw, 3)
    get_scan = load(scan_in, scan, 4)
    get_ow = load(out_w, ow, 5)
    get_conv.start()
    get_pw.start()
    get_sw.start()

    barrier = pltpu.get_barrier_semaphore()

    def partner(k):
        idx = lax.rem(me + k, total)
        return (g, idx // 2, idx % 2, 0), idx

    def greet(k, carry):
        pl.semaphore_signal(barrier, inc=1, device_id=partner(k)[0], device_id_type=MESH)
        return carry

    lax.fori_loop(1, total, greet, 0)
    pl.semaphore_wait(barrier, total - 1)

    def send(src, dst, ssem, rsem, where):
        return pltpu.make_async_remote_copy(
            src_ref=src, dst_ref=dst, send_sem=ssem, recv_sem=rsem, device_id=where, device_id_type=MESH
        )

    def tok_copy(half, blk, ssem, where):
        ref = tok.at[half, block_rows(blk)]
        return send(ref, ref, ssem, tok_recv.at[half, blk], where)

    def to_z(k):
        z_to = lax.rem(z + k, nz)
        return tok_copy(x, b, tok_z.at[k], (g, z_to * 2 + c, x, 0))

    def to_peer(k):
        blk = lax.rem(z + k, nz) * 2 + c
        return tok_copy(x, blk, tok_x.at[k], peer)

    def to_twin(h, k):
        blk = lax.rem(z + k, nz) * 2 + c
        return tok_copy((x + h) % 2, blk, tok_sib.at[h, k], twin)

    def got(half, blk):
        ref = tok.at[half, block_rows(blk)]
        send(ref, ref, tok_z.at[0], tok_recv.at[half, blk], peer).wait_recv()

    first.wait()
    to_peer(0).start()
    for k in range(1, nz):
        to_z(k).start()
    to_twin(0, 0).start()

    small[...] = jnp.zeros_like(small)
    small[0:8, :] = packed[0:8, :]
    for j in range(2 * wide // chan):
        gain_row[:, j * chan : (j + 1) * chan] = packed[8 + j : 9 + j, :]
    rates[...] = -jnp.exp(decay_log[...])

    def flip_small(i, carry):
        at = pl.ds(pl.multiple_of(i * LANES, LANES), LANES)
        small_t[at, :] = small[:, at].T
        return carry

    lax.fori_loop(0, nblk, flip_small, 0)
    squares[...] = jnp.zeros_like(squares)
    acc[...] = jnp.zeros_like(acc)
    pp[...] = jnp.zeros_like(pp)

    for k in range(1, nz):
        got(x, lax.rem(z + k, nz) * 2 + c)
        to_peer(k).start()
        to_twin(0, k).start()

    for h in range(2):
        half = (x + h) % 2
        if h == 1:
            for k in range(nz):
                got(half, lax.rem(z + k, nz) * 2 + c)
                to_twin(1, k).start()
        for k in range(nz):
            got(half, lax.rem(z + k, nz) * 2 + 1 - c)

        def scale(j, carry):
            at = pl.ds(pl.multiple_of(j * LANES, LANES), LANES)
            gain = gain_row[:, pl.ds(pl.multiple_of(half * wide + j * LANES, LANES), LANES)]
            v = tok[half, :, at].astype(F32)
            squares[...] += v * v
            scaled[:, at] = (v * gain).astype(BF16)
            return carry

        lax.fori_loop(0, wide // LANES, scale, 0)

        def project(j, carry):
            t = h * PARTS + j
            weight(t).wait()
            lhs = scaled[:, pl.ds(pl.multiple_of(j * kc, kc), kc)]
            slot = t % RING
            for w in range(2):
                acc[w] += jnp.dot(lhs, iw[slot, w], preferred_element_type=F32)

            @pl.when(t + RING < 2 * PARTS)
            def _():
                weight(t + RING).start()

            return carry

        lax.fori_loop(0, PARTS, project, 0)
        if h == 0:
            get_scan.start()
            get_ow.start()

    inv = lax.rsqrt(jnp.sum(squares[...], axis=1, keepdims=True) / (2.0 * wide) + 1e-06)
    get_conv.wait()

    def convolve(i, carry):
        at = pl.ds(pl.multiple_of(i * LANES, LANES), LANES)
        br = (acc[0, :, at] * inv).T.astype(BF16)
        branch[at, :] = br
        cols = small_t[at, :]
        v = br.astype(F32) * cols[:, 3:4]
        for k in range(3):
            v += conv[k, at, :].astype(F32) * cols[:, k : k + 1]
        a = silu(v + cols[:, 4:5]).astype(BF16).astype(F32)
        act[at, :] = a
        act_t[:, at] = a.T.astype(BF16)
        gt = (acc[1, :, at] * inv).T.astype(BF16).astype(F32)
        gate[at, :] = silu(gt)
        return carry

    lax.fori_loop(0, nblk, convolve, 0)
    put_conv = pltpu.make_async_copy(conv.at[pl.ds(1, 2)], conv_out.at[pl.ds(0, 2)], store_sem.at[0])
    put_branch = pltpu.make_async_copy(branch, conv_out.at[2], store_sem.at[1])
    put_conv.start()
    put_branch.start()

    get_pw.wait()
    width = pw.shape[0]
    terms = lax.dot_general(
        act_t[...], pw[...], (((1,), (1,)), ((), ())), preferred_element_type=F32
    ).astype(BF16)
    pp[0] = terms[:, 0:HALF].reshape(blocks, rows, HALF)
    dot_out[...] = jnp.zeros_like(dot_out)
    dot_out[:, 0 : width - HALF] = terms[:, HALF:width]
    pp[1] = dot_out[...].reshape(blocks, rows, HALF)

    def par_copy(k):
        where, idx = partner(k)
        return send(pp.at[idx % 2, idx // 2], prv.at[me], par_send.at[k], par_recv.at[me], where)

    def all_copy(k):
        where, idx = partner(k)
        ref = pall.at[x, b]
        return send(ref, ref, all_send.at[k], all_recv.at[me], where)

    def start_par(k, carry):
        par_copy(k).start()
        return carry

    lax.fori_loop(1, total, start_par, 0)

    def take_par(k, summed):
        where, idx = partner(k)
        send(prv.at[idx], prv.at[idx], par_send.at[0], par_recv.at[idx], where).wait_recv()
        return summed + prv[idx].astype(F32)

    summed = lax.fori_loop(1, total, take_par, pp[x, b].astype(F32))
    pall[x, b] = summed.astype(BF16)

    def start_all(k, carry):
        all_copy(k).start()
        return carry

    lax.fori_loop(1, total, start_all, 0)
    get_sw.wait()
    get_scan.wait()

    def take_all(k, carry):
        where, idx = partner(k)
        ref = pall.at[idx % 2, idx // 2]
        send(ref, ref, all_send.at[0], all_recv.at[idx], where).wait_recv()
        return carry

    lax.fori_loop(1, total, take_all, 0)

    one = pall[0].astype(F32).reshape(seqs, HALF)
    two = pall[1].astype(F32).reshape(seqs, HALF)
    rank = low.shape[1]
    extra = two[:, 0 : rank - HALF]
    norm = lax.rsqrt(
        (jnp.sum(one * one, axis=1, keepdims=True) + jnp.sum(extra * extra, axis=1, keepdims=True)) / rank
        + 1e-06
    )
    at_rank = 8 + 2 * wide // chan
    gains = packed[at_rank : at_rank + 1, 0:rank]
    low[:, 0:HALF] = (one * norm * gains[:, 0:HALF]).astype(BF16)
    low[:, HALF:rank] = (extra * norm * gains[:, HALF:rank]).astype(BF16)
    flipped = two[:, rank - HALF : rank - HALF + LANES].T
    states = inout.shape[1]
    for k in range(2):
        at = slice(k * states, (k + 1) * states)
        v = flipped[at]
        v = v * lax.rsqrt(jnp.mean(v * v, axis=0, keepdims=True) + 1e-06) * small_t[at, 7:8]
        inout[k] = v.astype(BF16).astype(F32)

    def head_copy(i):
        at = pl.ds(pl.multiple_of(x * chan + i * LANES, LANES), LANES)
        ref = heads.at[:, at]
        return send(ref, ref, head_send.at[i], head_recv.at[i], peer)

    def head_got(i):
        at = pl.ds(pl.multiple_of((1 - x) * chan + i * LANES, LANES), LANES)
        ref = heads.at[:, at]
        send(ref, ref, head_send.at[i], head_recv.at[i], peer).wait_recv()

    def put_scan(i):
        at = pl.ds(pl.multiple_of(i * LANES, LANES), LANES)
        return pltpu.make_async_copy(scan.at[at], scan_out.at[at], scan_sem.at[i])

    def advance(i, carry):
        base = pl.multiple_of(i * LANES, LANES)
        at = pl.ds(base, LANES)
        cols = small_t[at, :]
        raw = jnp.dot(low[...], sw[:, at], preferred_element_type=F32).T
        st = softplus(raw + cols[:, 5:6])
        step[...] = st
        drive[...] = st * act[at, :]
        decay = rates[:, at]

        def group(q, inner):
            rolled = pltpu.roll(decay, LANES - q * 8, 1)
            entry = inout[0]
            readout = inout[1]
            at8 = pl.ds(pl.multiple_of(q * 8, 8), 8)
            at_scan = pl.ds(pl.multiple_of(base + q * 8, 8), 8)
            times = step[at8, :]
            drives = drive[at8, :]
            olds = scan[at_scan]
            news = []
            sums = []
            for j in range(8):
                fade = jnp.exp(times[j : j + 1] * rolled[:, j : j + 1])
                state = fade * olds[j].astype(F32) + drives[j : j + 1] * entry
                news.append(state.astype(BF16)[None])
                sums.append(jnp.sum(state * readout, axis=0, keepdims=True))
            scan[at_scan] = jnp.concatenate(news, axis=0)
            step[at8, :] = jnp.concatenate(sums, axis=0)
            return inner

        lax.fori_loop(0, LANES // 8, group, 0)
        put_scan(i).start()
        out = (step[...] + cols[:, 6:7] * act[at, :]) * gate[at, :]
        heads[:, pl.ds(pl.multiple_of(x * chan + i * LANES, LANES), LANES)] = out.T.astype(BF16)
        head_copy(i).start()
        return carry

    lax.fori_loop(0, nblk, advance, 0)
    get_ow.wait()

    def wait_heads(i, carry):
        head_got(i)
        return carry

    lax.fori_loop(0, nblk, wait_heads, 0)

    def sib_copy(n):
        return send(part.at[n, :, 1 - c], sib.at[n], sib_send.at[n], sib_recv.at[n], twin)

    def far_copy(n, k):
        z_to = lax.rem(z + k, nz)
        return send(
            mine.at[n, z_to], far.at[n, k], far_send.at[n, k], far_recv.at[n, k], (g, z_to * 2 + c, x, 0)
        )

    for n in range(PARTS + 1):
        if n < PARTS:
            p = jnp.dot(heads[...], ow[:, n * kc : (n + 1) * kc], preferred_element_type=F32)
            part[n] = p.astype(BF16).reshape(nz, 2, rows, kc)
            sib_copy(n).start()
        if n > 0:
            m = n - 1
            sib_copy(m).wait_recv()
            mine[m] = (part[m, :, c].astype(F32) + sib[m].astype(F32)).astype(BF16)
            for k in range(1, nz):
                far_copy(m, k).start()

    for n in range(PARTS):
        v = mine[n, z].astype(F32)
        for k in range(1, nz):
            far_copy(n, k).wait_recv()
            v += far[n, k].astype(F32)
        at = slice(n * kc, (n + 1) * kc)
        own = tok[x, block_rows(b), at].astype(F32)
        mix[:, at] = (own + v).astype(BF16)
    put_mix = pltpu.make_async_copy(mix, mixed, store_sem.at[2])
    put_mix.start()

    for k in range(nz):
        to_peer(k).wait_send()
        to_twin(0, k).wait_send()
        to_twin(1, k).wait_send()
    for k in range(1, nz):
        to_z(k).wait_send()

    def drain(k, carry):
        par_copy(k).wait_send()
        all_copy(k).wait_send()
        return carry

    lax.fori_loop(1, total, drain, 0)

    def drain_blocks(i, carry):
        head_copy(i).wait_send()
        put_scan(i).wait()
        return carry

    lax.fori_loop(0, nblk, drain_blocks, 0)
    for n in range(PARTS):
        sib_copy(n).wait_send()
        for k in range(1, nz):
            far_copy(n, k).wait_send()
    put_conv.wait()
    put_branch.wait()
    put_mix.wait()


def fused(
    blocks,
    tokens,
    input_gain,
    in_weight,
    conv_weight,
    conv_bias,
    param_weight,
    step_gain,
    entry_gain,
    readout_gain,
    step_weight,
    step_bias,
    decay_log,
    skip_gain,
    out_weight,
    conv_state,
    scan_state,
):
    rows, wide = tokens.shape
    seqs = rows * blocks
    chan = in_weight.shape[2]
    rank = step_gain.shape[0]
    states = entry_gain.shape[0]
    nz = blocks // 2
    kc = wide // PARTS
    nblk = chan // LANES
    total = 2 * blocks
    vm = pl.BlockSpec(memory_space=pltpu.VMEM)
    hbm = pl.BlockSpec(memory_space=pl.ANY)
    dma = pltpu.SemaphoreType.DMA
    v = pltpu.VMEM
    scratch = [
        v((2, seqs, wide), BF16),
        v((seqs, wide), BF16),
        v((seqs, LANES), F32),
        v((RING, 2, kc, chan), BF16),
        v((2, seqs, chan), F32),
        v(param_weight.shape[::-1], BF16),
        v(step_weight.shape, BF16),
        v(out_weight.shape, BF16),
        v(conv_state.shape, BF16),
        v((chan, seqs), BF16),
        v(scan_state.shape, BF16),
        v((1, 2 * wide), F32),
        v((LANES, chan), F32),
        v((chan, LANES), F32),
        v((states, chan), F32),
        v((chan, seqs), F32),
        v((seqs, chan), BF16),
        v((chan, seqs), F32),
        v((LANES, seqs), F32),
        v((LANES, seqs), F32),
        v((2, blocks, rows, HALF), BF16),
        v((total, rows, HALF), BF16),
        v((2, blocks, rows, HALF), BF16),
        v((seqs, rank), BF16),
        v((2, states, seqs), F32),
        v((seqs, HALF), BF16),
        v((seqs, 2 * chan), BF16),
        v((PARTS, nz, 2, rows, kc), BF16),
        v((PARTS, nz, rows, kc), BF16),
        v((PARTS, nz, rows, kc), BF16),
        v((PARTS, nz, rows, kc), BF16),
        v((rows, wide), BF16),
        dma((6,)),
        dma((RING,)),
        dma((3,)),
        dma((nblk,)),
        dma((2, blocks)),
        dma((nz,)),
        dma((nz,)),
        dma((2, nz)),
        dma((total,)),
        dma((total,)),
        dma((total,)),
        dma((total,)),
        dma((nblk,)),
        dma((nblk,)),
        dma((PARTS,)),
        dma((PARTS,)),
        dma((PARTS, nz)),
        dma((PARTS, nz)),
    ]
    gains = jnp.concatenate([entry_gain, readout_gain]).astype(F32)
    packed = jnp.concatenate(
        [
            conv_weight.astype(F32),
            conv_bias.astype(F32)[None],
            step_bias[None],
            skip_gain[None],
            jnp.pad(gains, (0, chan - 2 * states))[None],
            input_gain.astype(F32).reshape(2 * wide // chan, chan),
            jnp.pad(step_gain.astype(F32), (0, chan - rank))[None],
        ],
        axis=0,
    )
    return pl.pallas_call(
        functools.partial(kernel, blocks),
        out_shape=(
            jax.ShapeDtypeStruct(tokens.shape, BF16),
            jax.ShapeDtypeStruct(conv_state.shape, BF16),
            jax.ShapeDtypeStruct(scan_state.shape, BF16),
        ),
        in_specs=[hbm, vm, hbm, hbm, hbm, vm, hbm, hbm, hbm],
        out_specs=(hbm, hbm, hbm),
        scratch_shapes=scratch,
        compiler_params=pltpu.CompilerParams(
            collective_id=0, has_side_effects=True, vmem_limit_bytes=62 * 1024 * 1024
        ),
    )(
        tokens,
        packed,
        in_weight,
        param_weight.T,
        step_weight,
        decay_log,
        out_weight,
        conv_state,
        scan_state,
    )


def fits(mesh, tokens, in_weight, step_gain, entry_gain, conv_weight):
    rows, wide = tokens.shape
    width = step_gain.shape[0] + 2 * entry_gain.shape[0]
    return (
        mesh.shape["sub"] == 1
        and mesh.shape["red"] == 2
        and mesh.shape["blk"] % 2 == 0
        and rows == 16
        and rows * mesh.shape["blk"] == LANES
        and in_weight.shape[2] % LANES == 0
        and wide % (PARTS * LANES) == 0
        and in_weight.shape[2] >= step_gain.shape[0]
        and 2 * wide % in_weight.shape[2] == 0
        and HALF < step_gain.shape[0] == HALF + LANES
        and width <= 2 * HALF
        and entry_gain.shape[0] == 16
        and conv_weight.shape[0] == 4
    )


def solution(mesh):
    def chosen(*args):
        if fits(mesh, args[0], args[2], args[6], args[7], args[3]):
            return fused(mesh.shape["blk"], *args)
        return body(*args)

    placed = (
        P(("grp", "blk"), ("red", "sub")),
        P(),
        P(None, None, ("blk", "red", "sub")),
        P(None, ("blk", "red", "sub")),
        P(("blk", "red", "sub")),
        P(("blk", "red", "sub"), None),
        P(),
        P(),
        P(),
        P(None, ("blk", "red", "sub")),
        P(("blk", "red", "sub")),
        P(None, ("blk", "red", "sub")),
        P(("blk", "red", "sub")),
        P("blk", ("red", "sub")),
        P(None, ("blk", "red", "sub"), "grp"),
        P(("blk", "red", "sub"), None, "grp"),
    )
    return jax.shard_map(
        chosen,
        mesh=mesh,
        in_specs=placed,
        out_specs=(
            P(("grp", "blk"), ("red", "sub")),
            P(None, ("blk", "red", "sub"), "grp"),
            P(("blk", "red", "sub"), None, "grp"),
        ),
        check_vma=False,
    )
```

```python
import functools
import jax
import jax.numpy as jnp
from jax import lax
from jax.experimental import pallas as pl
from jax.experimental.pallas import tpu as pltpu
from jax.sharding import PartitionSpec as P


def contract(left, right, dims):
    return lax.dot_general(
        left,
        right,
        (dims, ((), ())),
        preferred_element_type=jnp.float32,
    )


def normalize(matrix, gain):
    return (
        matrix
        * lax.rsqrt(jnp.mean(matrix * matrix, axis=0, keepdims=True) + 1e-06)
        * gain.astype(jnp.float32)[:, None]
    )


def prenorm(rows_in, input_gain):
    wide = rows_in.astype(jnp.float32)
    scaled = wide * lax.rsqrt(jnp.mean(wide * wide, axis=1, keepdims=True) + 1e-06)
    return (scaled * input_gain.astype(jnp.float32)[None, :]).astype(jnp.bfloat16)


def split_params(summed, step_gain, entry_gain, readout_gain):
    width_low = step_gain.shape[0]
    width_state = entry_gain.shape[0]
    step_low = normalize(summed[:width_low], step_gain).astype(jnp.bfloat16)
    entry = normalize(summed[width_low : width_low + width_state], entry_gain).astype(jnp.bfloat16)
    readout = normalize(summed[width_low + width_state :], readout_gain).astype(jnp.bfloat16)
    return (step_low, entry, readout)


def body(
    tokens,
    input_gain,
    in_weight,
    conv_weight,
    conv_bias,
    param_weight,
    step_gain,
    entry_gain,
    readout_gain,
    step_weight,
    step_bias,
    decay_log,
    skip_gain,
    out_weight,
    conv_state,
    scan_state,
):
    all_rows = lax.all_gather(tokens, "blk", axis=0, tiled=True)
    full_rows = lax.all_gather(all_rows, ("red", "sub"), axis=1, tiled=True)
    row_piece = prenorm(full_rows, input_gain)
    first = contract(in_weight[0], row_piece, ((0,), (1,)))
    second = contract(in_weight[1], row_piece, ((0,), (1,)))
    projected = jnp.stack([first, second], axis=0)
    branch = projected[0].astype(jnp.bfloat16)
    gating = projected[1].astype(jnp.bfloat16)
    window = jnp.concatenate([conv_state, branch[None]], axis=0)
    new_conv = window[1:]
    convolved = (
        jnp.sum(window.astype(jnp.float32) * conv_weight.astype(jnp.float32)[:, :, None], axis=0)
        + conv_bias.astype(jnp.float32)[:, None]
    )
    activated = jax.nn.silu(convolved).astype(jnp.bfloat16)
    param_terms = contract(param_weight, activated, ((0,), (0,)))
    summed = lax.psum(param_terms, ("blk", "red", "sub"))
    step_low, entry, readout = split_params(summed, step_gain, entry_gain, readout_gain)
    step = jax.nn.softplus(contract(step_weight, step_low, ((0,), (0,))) + step_bias[:, None])
    active_wide = activated.astype(jnp.float32)
    rates = (-jnp.exp(decay_log)).T
    state = jnp.exp(step[:, None, :] * rates[:, :, None]) * scan_state.astype(jnp.float32)
    state = state + (step * active_wide)[:, None, :] * entry.astype(jnp.float32)[None, :, :]
    gated = (
        jnp.sum(state * readout.astype(jnp.float32)[None, :, :], axis=1)
        + skip_gain[:, None] * active_wide
    )
    gated = (gated * jax.nn.silu(gating.astype(jnp.float32))).astype(jnp.bfloat16)
    gathered = lax.all_gather(gated, ("red", "sub"), axis=0, tiled=True)
    output = lax.psum_scatter(
        contract(gathered, out_weight, ((0,), (0,))).astype(jnp.bfloat16),
        "blk",
        scatter_dimension=0,
        tiled=True,
    ).astype(jnp.float32)
    mixed = (tokens.astype(jnp.float32) + output).astype(jnp.bfloat16)
    return (mixed, new_conv, state.astype(jnp.bfloat16))


MESH = pl.DeviceIdType.MESH
F32 = jnp.float32
BF16 = jnp.bfloat16
LANES = 128
HALF = 384
RING = 6
PARTS = 4


def silu(v):
    return v / (1.0 + jnp.exp(-v))


def softplus(v):
    return jnp.maximum(v, 0.0) + jnp.log1p(jnp.exp(-jnp.abs(v)))


def kernel(
    blocks,
    tokens,
    packed,
    in_w,
    par_w,
    step_w,
    decay_log,
    out_w,
    conv_in,
    scan_in,
    mixed,
    conv_out,
    scan_out,
    tok,
    scaled,
    squares,
    iw,
    acc,
    pw,
    sw,
    ow,
    conv,
    branch,
    scan,
    gain_row,
    small,
    small_t,
    rates,
    act,
    act_t,
    gate,
    step,
    drive,
    pp,
    prv,
    pall,
    low,
    inout,
    dot_out,
    heads,
    part,
    sib,
    mine,
    far,
    mix,
    load_sem,
    iw_sem,
    store_sem,
    scan_sem,
    tok_recv,
    tok_z,
    tok_x,
    tok_sib,
    par_send,
    par_recv,
    all_send,
    all_recv,
    head_send,
    head_recv,
    sib_send,
    sib_recv,
    far_send,
    far_recv,
):
    g = lax.axis_index("grp")
    b = lax.axis_index("blk")
    x = lax.axis_index("red")
    z = b // 2
    c = b % 2
    nz = blocks // 2
    me = b * 2 + x
    total = blocks * 2
    rows = tokens.shape[0]
    wide = tokens.shape[1]
    seqs = rows * blocks
    chan = act.shape[0]
    kc = wide // PARTS
    nblk = chan // LANES
    twin = (g, b + 1 - 2 * c, x, 0)
    peer = (g, b, 1 - x, 0)

    def load(src, dst, at):
        return pltpu.make_async_copy(src, dst, load_sem.at[at])

    def weight(t):
        h, j = t // PARTS, t % PARTS
        start = ((x + h) % 2) * wide + j * kc
        return pltpu.make_async_copy(
            in_w.at[:, pl.ds(pl.multiple_of(start, kc), kc), :],
            iw.at[t % RING],
            iw_sem.at[t % RING],
        )

    def block_rows(at):
        return pl.ds(pl.multiple_of(at * rows, rows), rows)

    first = load(tokens, tok.at[x, block_rows(b)], 0)
    first.start()
    for t in range(RING):
        weight(t).start()
    get_conv = load(conv_in, conv, 1)
    get_pw = load(par_w, pw, 2)
    get_sw = load(step_w, sw, 3)
    get_scan = load(scan_in, scan, 4)
    get_ow = load(out_w, ow, 5)
    get_conv.start()
    get_pw.start()
    get_sw.start()

    barrier = pltpu.get_barrier_semaphore()

    def partner(k):
        idx = lax.rem(me + k, total)
        return (g, idx // 2, idx % 2, 0), idx

    def greet(k, carry):
        pl.semaphore_signal(barrier, inc=1, device_id=partner(k)[0], device_id_type=MESH)
        return carry

    lax.fori_loop(1, total, greet, 0)
    pl.semaphore_wait(barrier, total - 1)

    def send(src, dst, ssem, rsem, where):
        return pltpu.make_async_remote_copy(
            src_ref=src, dst_ref=dst, send_sem=ssem, recv_sem=rsem, device_id=where, device_id_type=MESH
        )

    def tok_copy(half, blk, ssem, where):
        ref = tok.at[half, block_rows(blk)]
        return send(ref, ref, ssem, tok_recv.at[half, blk], where)

    def to_z(k):
        z_to = lax.rem(z + k, nz)
        return tok_copy(x, b, tok_z.at[k], (g, z_to * 2 + c, x, 0))

    def to_peer(k):
        blk = lax.rem(z + k, nz) * 2 + c
        return tok_copy(x, blk, tok_x.at[k], peer)

    def to_twin(h, k):
        blk = lax.rem(z + k, nz) * 2 + c
        return tok_copy((x + h) % 2, blk, tok_sib.at[h, k], twin)

    def got(half, blk):
        ref = tok.at[half, block_rows(blk)]
        send(ref, ref, tok_z.at[0], tok_recv.at[half, blk], peer).wait_recv()

    first.wait()
    to_peer(0).start()
    for k in range(1, nz):
        to_z(k).start()
    to_twin(0, 0).start()

    small[...] = jnp.zeros_like(small)
    small[0:8, :] = packed[0:8, :]
    for j in range(2 * wide // chan):
        gain_row[:, j * chan : (j + 1) * chan] = packed[8 + j : 9 + j, :]
    rates[...] = -jnp.exp(decay_log[...])

    def flip_small(i, carry):
        at = pl.ds(pl.multiple_of(i * LANES, LANES), LANES)
        small_t[at, :] = small[:, at].T
        return carry

    lax.fori_loop(0, nblk, flip_small, 0)
    squares[...] = jnp.zeros_like(squares)
    acc[...] = jnp.zeros_like(acc)
    pp[...] = jnp.zeros_like(pp)

    for k in range(1, nz):
        got(x, lax.rem(z + k, nz) * 2 + c)
        to_peer(k).start()
        to_twin(0, k).start()

    for h in range(2):
        half = (x + h) % 2
        if h == 1:
            for k in range(nz):
                got(half, lax.rem(z + k, nz) * 2 + c)
                to_twin(1, k).start()
        for k in range(nz):
            got(half, lax.rem(z + k, nz) * 2 + 1 - c)

        def scale(j, carry):
            at = pl.ds(pl.multiple_of(j * LANES, LANES), LANES)
            gain = gain_row[:, pl.ds(pl.multiple_of(half * wide + j * LANES, LANES), LANES)]
            v = tok[half, :, at].astype(F32)
            squares[...] += v * v
            scaled[:, at] = (v * gain).astype(BF16)
            return carry

        lax.fori_loop(0, wide // LANES, scale, 0)

        def project(j, carry):
            t = h * PARTS + j
            weight(t).wait()
            lhs = scaled[:, pl.ds(pl.multiple_of(j * kc, kc), kc)]
            slot = t % RING
            for w in range(2):
                acc[w] += jnp.dot(lhs, iw[slot, w], preferred_element_type=F32)

            @pl.when(t + RING < 2 * PARTS)
            def _():
                weight(t + RING).start()

            return carry

        lax.fori_loop(0, PARTS, project, 0)
        if h == 0:
            get_scan.start()
            get_ow.start()

    inv = lax.rsqrt(jnp.sum(squares[...], axis=1, keepdims=True) / (2.0 * wide) + 1e-06)
    get_conv.wait()

    def convolve(i, carry):
        at = pl.ds(pl.multiple_of(i * LANES, LANES), LANES)
        br = (acc[0, :, at] * inv).T.astype(BF16)
        branch[at, :] = br
        cols = small_t[at, :]
        v = br.astype(F32) * cols[:, 3:4]
        for k in range(3):
            v += conv[k, at, :].astype(F32) * cols[:, k : k + 1]
        a = silu(v + cols[:, 4:5]).astype(BF16).astype(F32)
        act[at, :] = a
        act_t[:, at] = a.T.astype(BF16)
        gt = (acc[1, :, at] * inv).T.astype(BF16).astype(F32)
        gate[at, :] = silu(gt)
        return carry

    lax.fori_loop(0, nblk, convolve, 0)
    put_conv = pltpu.make_async_copy(conv.at[pl.ds(1, 2)], conv_out.at[pl.ds(0, 2)], store_sem.at[0])
    put_branch = pltpu.make_async_copy(branch, conv_out.at[2], store_sem.at[1])
    put_conv.start()
    put_branch.start()

    get_pw.wait()
    width = pw.shape[0]
    terms = lax.dot_general(
        act_t[...], pw[...], (((1,), (1,)), ((), ())), preferred_element_type=F32
    ).astype(BF16)
    pp[0] = terms[:, 0:HALF].reshape(blocks, rows, HALF)
    dot_out[...] = jnp.zeros_like(dot_out)
    dot_out[:, 0 : width - HALF] = terms[:, HALF:width]
    pp[1] = dot_out[...].reshape(blocks, rows, HALF)

    def par_copy(k):
        where, idx = partner(k)
        return send(pp.at[idx % 2, idx // 2], prv.at[me], par_send.at[k], par_recv.at[me], where)

    def all_copy(k):
        where, idx = partner(k)
        ref = pall.at[x, b]
        return send(ref, ref, all_send.at[k], all_recv.at[me], where)

    def start_par(k, carry):
        par_copy(k).start()
        return carry

    lax.fori_loop(1, total, start_par, 0)

    def take_par(k, summed):
        where, idx = partner(k)
        send(prv.at[idx], prv.at[idx], par_send.at[0], par_recv.at[idx], where).wait_recv()
        return summed + prv[idx].astype(F32)

    summed = lax.fori_loop(1, total, take_par, pp[x, b].astype(F32))
    pall[x, b] = summed.astype(BF16)

    def start_all(k, carry):
        all_copy(k).start()
        return carry

    lax.fori_loop(1, total, start_all, 0)
    get_sw.wait()
    get_scan.wait()

    def take_all(k, carry):
        where, idx = partner(k)
        ref = pall.at[idx % 2, idx // 2]
        send(ref, ref, all_send.at[0], all_recv.at[idx], where).wait_recv()
        return carry

    lax.fori_loop(1, total, take_all, 0)

    one = pall[0].astype(F32).reshape(seqs, HALF)
    two = pall[1].astype(F32).reshape(seqs, HALF)
    rank = low.shape[1]
    extra = two[:, 0 : rank - HALF]
    norm = lax.rsqrt(
        (jnp.sum(one * one, axis=1, keepdims=True) + jnp.sum(extra * extra, axis=1, keepdims=True)) / rank
        + 1e-06
    )
    at_rank = 8 + 2 * wide // chan
    gains = packed[at_rank : at_rank + 1, 0:rank]
    low[:, 0:HALF] = (one * norm * gains[:, 0:HALF]).astype(BF16)
    low[:, HALF:rank] = (extra * norm * gains[:, HALF:rank]).astype(BF16)
    flipped = two[:, rank - HALF : rank - HALF + LANES].T
    states = inout.shape[1]
    for k in range(2):
        at = slice(k * states, (k + 1) * states)
        v = flipped[at]
        v = v * lax.rsqrt(jnp.mean(v * v, axis=0, keepdims=True) + 1e-06) * small_t[at, 7:8]
        inout[k] = v.astype(BF16).astype(F32)

    def head_copy(i):
        at = pl.ds(pl.multiple_of(x * chan + i * LANES, LANES), LANES)
        ref = heads.at[:, at]
        return send(ref, ref, head_send.at[i], head_recv.at[i], peer)

    def head_got(i):
        at = pl.ds(pl.multiple_of((1 - x) * chan + i * LANES, LANES), LANES)
        ref = heads.at[:, at]
        send(ref, ref, head_send.at[i], head_recv.at[i], peer).wait_recv()

    def put_scan(i):
        at = pl.ds(pl.multiple_of(i * LANES, LANES), LANES)
        return pltpu.make_async_copy(scan.at[at], scan_out.at[at], scan_sem.at[i])

    def advance(i, carry):
        base = pl.multiple_of(i * LANES, LANES)
        at = pl.ds(base, LANES)
        cols = small_t[at, :]
        raw = jnp.dot(low[...], sw[:, at], preferred_element_type=F32).T
        st = softplus(raw + cols[:, 5:6])
        step[...] = st
        drive[...] = st * act[at, :]
        decay = rates[:, at]
        place = lax.broadcasted_iota(jnp.int32, (8, seqs), 0)

        def group(q, inner):
            rolled = pltpu.roll(decay, LANES - q * 8, 1)
            entry = inout[0]
            readout = inout[1]
            at8 = pl.ds(pl.multiple_of(q * 8, 8), 8)
            at_scan = pl.ds(pl.multiple_of(base + q * 8, 8), 8)
            times = step[at8, :]
            drives = drive[at8, :]
            olds = scan[at_scan]
            news = []
            sums = []
            for j in range(8):
                fade = jnp.exp(times[j : j + 1] * rolled[:, j : j + 1])
                state = fade * olds[j].astype(F32) + drives[j : j + 1] * entry
                news.append(state.astype(BF16)[None])
                seen = state * readout
                sums.append(seen[0:8] + seen[8:16])
            scan[at_scan] = jnp.concatenate(news, axis=0)
            for shift in (1, 2, 4):
                keep = (place // shift) % 2 == 0
                sums = [
                    jnp.where(keep, left, right) + pltpu.roll(jnp.where(keep, right, left), shift, 0)
                    for left, right in zip(sums[0::2], sums[1::2])
                ]
            step[at8, :] = sums[0]
            return inner

        lax.fori_loop(0, LANES // 8, group, 0)
        put_scan(i).start()
        out = (step[...] + cols[:, 6:7] * act[at, :]) * gate[at, :]
        heads[:, pl.ds(pl.multiple_of(x * chan + i * LANES, LANES), LANES)] = out.T.astype(BF16)
        head_copy(i).start()
        return carry

    lax.fori_loop(0, nblk, advance, 0)
    get_ow.wait()

    def wait_heads(i, carry):
        head_got(i)
        return carry

    lax.fori_loop(0, nblk, wait_heads, 0)

    def sib_copy(n):
        return send(part.at[n, :, 1 - c], sib.at[n], sib_send.at[n], sib_recv.at[n], twin)

    def far_copy(n, k):
        z_to = lax.rem(z + k, nz)
        return send(
            mine.at[n, z_to], far.at[n, k], far_send.at[n, k], far_recv.at[n, k], (g, z_to * 2 + c, x, 0)
        )

    for n in range(PARTS + 1):
        if n < PARTS:
            p = jnp.dot(heads[...], ow[:, n * kc : (n + 1) * kc], preferred_element_type=F32)
            part[n] = p.astype(BF16).reshape(nz, 2, rows, kc)
            sib_copy(n).start()
        if n > 0:
            m = n - 1
            sib_copy(m).wait_recv()
            mine[m] = (part[m, :, c].astype(F32) + sib[m].astype(F32)).astype(BF16)
            for k in range(1, nz):
                far_copy(m, k).start()

    for n in range(PARTS):
        v = mine[n, z].astype(F32)
        for k in range(1, nz):
            far_copy(n, k).wait_recv()
            v += far[n, k].astype(F32)
        at = slice(n * kc, (n + 1) * kc)
        own = tok[x, block_rows(b), at].astype(F32)
        mix[:, at] = (own + v).astype(BF16)
    put_mix = pltpu.make_async_copy(mix, mixed, store_sem.at[2])
    put_mix.start()

    for k in range(nz):
        to_peer(k).wait_send()
        to_twin(0, k).wait_send()
        to_twin(1, k).wait_send()
    for k in range(1, nz):
        to_z(k).wait_send()

    def drain(k, carry):
        par_copy(k).wait_send()
        all_copy(k).wait_send()
        return carry

    lax.fori_loop(1, total, drain, 0)

    def drain_blocks(i, carry):
        head_copy(i).wait_send()
        put_scan(i).wait()
        return carry

    lax.fori_loop(0, nblk, drain_blocks, 0)
    for n in range(PARTS):
        sib_copy(n).wait_send()
        for k in range(1, nz):
            far_copy(n, k).wait_send()
    put_conv.wait()
    put_branch.wait()
    put_mix.wait()


def fused(
    blocks,
    tokens,
    input_gain,
    in_weight,
    conv_weight,
    conv_bias,
    param_weight,
    step_gain,
    entry_gain,
    readout_gain,
    step_weight,
    step_bias,
    decay_log,
    skip_gain,
    out_weight,
    conv_state,
    scan_state,
):
    rows, wide = tokens.shape
    seqs = rows * blocks
    chan = in_weight.shape[2]
    rank = step_gain.shape[0]
    states = entry_gain.shape[0]
    nz = blocks // 2
    kc = wide // PARTS
    nblk = chan // LANES
    total = 2 * blocks
    vm = pl.BlockSpec(memory_space=pltpu.VMEM)
    hbm = pl.BlockSpec(memory_space=pl.ANY)
    dma = pltpu.SemaphoreType.DMA
    v = pltpu.VMEM
    scratch = [
        v((2, seqs, wide), BF16),
        v((seqs, wide), BF16),
        v((seqs, LANES), F32),
        v((RING, 2, kc, chan), BF16),
        v((2, seqs, chan), F32),
        v(param_weight.shape[::-1], BF16),
        v(step_weight.shape, BF16),
        v(out_weight.shape, BF16),
        v(conv_state.shape, BF16),
        v((chan, seqs), BF16),
        v(scan_state.shape, BF16),
        v((1, 2 * wide), F32),
        v((LANES, chan), F32),
        v((chan, LANES), F32),
        v((states, chan), F32),
        v((chan, seqs), F32),
        v((seqs, chan), BF16),
        v((chan, seqs), F32),
        v((LANES, seqs), F32),
        v((LANES, seqs), F32),
        v((2, blocks, rows, HALF), BF16),
        v((total, rows, HALF), BF16),
        v((2, blocks, rows, HALF), BF16),
        v((seqs, rank), BF16),
        v((2, states, seqs), F32),
        v((seqs, HALF), BF16),
        v((seqs, 2 * chan), BF16),
        v((PARTS, nz, 2, rows, kc), BF16),
        v((PARTS, nz, rows, kc), BF16),
        v((PARTS, nz, rows, kc), BF16),
        v((PARTS, nz, rows, kc), BF16),
        v((rows, wide), BF16),
        dma((6,)),
        dma((RING,)),
        dma((3,)),
        dma((nblk,)),
        dma((2, blocks)),
        dma((nz,)),
        dma((nz,)),
        dma((2, nz)),
        dma((total,)),
        dma((total,)),
        dma((total,)),
        dma((total,)),
        dma((nblk,)),
        dma((nblk,)),
        dma((PARTS,)),
        dma((PARTS,)),
        dma((PARTS, nz)),
        dma((PARTS, nz)),
    ]
    gains = jnp.concatenate([entry_gain, readout_gain]).astype(F32)
    packed = jnp.concatenate(
        [
            conv_weight.astype(F32),
            conv_bias.astype(F32)[None],
            step_bias[None],
            skip_gain[None],
            jnp.pad(gains, (0, chan - 2 * states))[None],
            input_gain.astype(F32).reshape(2 * wide // chan, chan),
            jnp.pad(step_gain.astype(F32), (0, chan - rank))[None],
        ],
        axis=0,
    )
    return pl.pallas_call(
        functools.partial(kernel, blocks),
        out_shape=(
            jax.ShapeDtypeStruct(tokens.shape, BF16),
            jax.ShapeDtypeStruct(conv_state.shape, BF16),
            jax.ShapeDtypeStruct(scan_state.shape, BF16),
        ),
        in_specs=[hbm, vm, hbm, hbm, hbm, vm, hbm, hbm, hbm],
        out_specs=(hbm, hbm, hbm),
        scratch_shapes=scratch,
        compiler_params=pltpu.CompilerParams(
            collective_id=0, has_side_effects=True, vmem_limit_bytes=62 * 1024 * 1024
        ),
    )(
        tokens,
        packed,
        in_weight,
        param_weight.T,
        step_weight,
        decay_log,
        out_weight,
        conv_state,
        scan_state,
    )


def fits(mesh, tokens, in_weight, step_gain, entry_gain, conv_weight):
    rows, wide = tokens.shape
    width = step_gain.shape[0] + 2 * entry_gain.shape[0]
    return (
        mesh.shape["sub"] == 1
        and mesh.shape["red"] == 2
        and mesh.shape["blk"] % 2 == 0
        and rows == 16
        and rows * mesh.shape["blk"] == LANES
        and in_weight.shape[2] % LANES == 0
        and wide % (PARTS * LANES) == 0
        and in_weight.shape[2] >= step_gain.shape[0]
        and 2 * wide % in_weight.shape[2] == 0
        and HALF < step_gain.shape[0] == HALF + LANES
        and width <= 2 * HALF
        and entry_gain.shape[0] == 16
        and conv_weight.shape[0] == 4
    )


def solution(mesh):
    def chosen(*args):
        if fits(mesh, args[0], args[2], args[6], args[7], args[3]):
            return fused(mesh.shape["blk"], *args)
        return body(*args)

    placed = (
        P(("grp", "blk"), ("red", "sub")),
        P(),
        P(None, None, ("blk", "red", "sub")),
        P(None, ("blk", "red", "sub")),
        P(("blk", "red", "sub")),
        P(("blk", "red", "sub"), None),
        P(),
        P(),
        P(),
        P(None, ("blk", "red", "sub")),
        P(("blk", "red", "sub")),
        P(None, ("blk", "red", "sub")),
        P(("blk", "red", "sub")),
        P("blk", ("red", "sub")),
        P(None, ("blk", "red", "sub"), "grp"),
        P(("blk", "red", "sub"), None, "grp"),
    )
    return jax.shard_map(
        chosen,
        mesh=mesh,
        in_specs=placed,
        out_specs=(
            P(("grp", "blk"), ("red", "sub")),
            P(None, ("blk", "red", "sub"), "grp"),
            P(("blk", "red", "sub"), None, "grp"),
        ),
        check_vma=False,
    )
```
